32 devices in a mesh: grp: 2 (over x), site: 16 (over z, y, core).
Axes of the slice: x: 2, y: 2, z: 4, core: 2. Of those that a mesh axis runs over, the one named last changes fastest.
Arguments:
- psi: bfloat16 [128, 128, 128], P(('grp', 'site')), parts along dimension 0, may hold values from -6 to 6
- left_env: bfloat16 [128, 34, 128, 128], P(('grp', 'site')), parts along dimension 0, may hold values from -1 to 2
- right_env: bfloat16 [128, 34, 128, 128], P(('grp', 'site')), parts along dimension 0, may hold values from -2 to 2
- mpo_shift: int32 [34], replicated, may hold values from -1 to 1
- block_sizes: int32 [128, 2], P(('grp', 'site')), parts along dimension 0, may hold values from 64 to 128
Outputs:
- krylov: bfloat16 [128, 128, 128], P(('grp', 'site')), parts along dimension 0
- image: bfloat16 [128, 128, 128], P(('grp', 'site')), parts along dimension 0
- coefficients: float32 [10], P('grp'), parts along dimension 0
The draws below stay inside these ranges and needn't reach their ends.
There are 2 independent parts, one for each index of `grp`. The reference program is written for one: setup_inputs(seed, part) draws one part's arguments, and reference() takes and returns one part's arrays. A program takes and returns all parts, laid end to end along the dimension named above; an argument that names none is the same for every part. Nothing has to cross between parts.
Inputs may be any that keep to these rules, and one draw needn't show every extreme that they name: `mpo_shift`: each MPO index moves the sector by -1, 0 or +1.
All inputs are finite; a program needn't handle non-finite values.
Results may differ from the reference program's by a relative error of at most 0.013.
Values may be sent and summed in bfloat16 or wider, within the bound.
A program may use at most 64 MiB of HBM per device.

```python
import jax
import jax.numpy as jnp
from jax import lax

BS = 128
W = 34
NL = 64


def draw_left_env(key, part):
    key = jax.random.fold_in(key, 11)
    noise_key, diag_key = jax.random.split(key, 2)
    base = (BS * W) ** (-0.5)
    ladder = jnp.arange(NL, dtype=jnp.float32) / max(NL - 1, 1) - 0.5
    unit = jnp.eye(BS, dtype=jnp.bool_)[None, None]
    entries = jnp.clip(jax.random.normal(noise_key, (NL, W, BS, BS), jnp.float32), -6.0, 6.0)
    ramp = jnp.exp(ladder * jnp.log(5.0))
    diagonal = jax.random.uniform(diag_key, (NL, W, BS, 1), jnp.float32, 0.2, 0.4)
    scaled = entries * base
    full = jnp.where(unit, scaled + diagonal, scaled)
    return (full * ramp[:, None, None, None]).astype(jnp.bfloat16)


def draw_right_env(key, part):
    key = jax.random.fold_in(key, 13)
    noise_key, diag_key = jax.random.split(key)
    base = BS ** (-0.5)
    unit = jnp.eye(BS, dtype=jnp.bool_)[None, None]
    entries = jnp.clip(jax.random.normal(noise_key, (NL, W, BS, BS), jnp.float32), -6.0, 6.0)
    diagonal = jax.random.uniform(diag_key, (NL, W, BS, 1), jnp.float32, 0.2, 0.4)
    scaled = entries * base
    return jnp.where(unit, scaled + diagonal, scaled).astype(jnp.bfloat16)


def place_ends(values, own_key, low, top_value):
    longest = values.shape.index(max(values.shape))
    spots = []
    for shift in (0, 1):
        where = [jax.random.randint(jax.random.fold_in(own_key, axis), (), 0, length) for axis, length in enumerate(values.shape)]
        where[longest] = (where[longest] + shift) % values.shape[longest]
        spots.append(tuple(where))
    return values.at[spots[0]].set(low).at[spots[1]].set(top_value)


def steps_of(own_key, dims, cuts, least, largest):
    factor_of = 1.0
    for axis_at, shards_of in cuts:
        draws = jax.random.uniform(jax.random.fold_in(jax.random.fold_in(own_key, 6), axis_at), (shards_of,), jnp.float32, least / len(cuts), largest / len(cuts))
        factor_of = factor_of * jnp.repeat(jnp.exp(draws), dims[axis_at] // shards_of).reshape((-1,) + (1,) * (len(dims) - 1 - axis_at))
    return factor_of


def centred(stream_key, shape, deviation, bound, shards=(), kind=jnp.bfloat16):
    factor_of = steps_of(stream_key, shape, shards, -0.22, 0.18) if shards else 1.0
    values = jax.random.normal(stream_key, shape, jnp.float32) * deviation * factor_of
    return jnp.minimum(jnp.maximum(values, -bound), bound).astype(kind)


def setup_inputs(seed: int = 0, part: int = 0) -> dict:
    arg_keys = jax.random.split(jax.random.key(seed), 6)
    part_keys = jax.random.split(jax.random.fold_in(arg_keys[5], part), 6)
    return {
        "psi": centred(part_keys[0], (NL, BS, BS), 1.0, 6.0, ((0, 16),)),
        "left_env": draw_left_env(jax.random.fold_in(jax.random.fold_in(arg_keys[5], part), 71), part),
        "right_env": draw_right_env(jax.random.fold_in(jax.random.fold_in(arg_keys[5], part), 71), part),
        "mpo_shift": place_ends(jax.random.randint(arg_keys[3], (W,), -1, 2), jax.random.fold_in(arg_keys[3], 1), -1, 1).astype(jnp.int32),
        "block_sizes": place_ends(jax.random.randint(part_keys[4], (NL, 2), BS // 2, BS + 1), jax.random.fold_in(part_keys[4], 1), BS // 2, BS).astype(jnp.int32),
    }


def live_of(block_sizes):
    positions = jnp.arange(BS, dtype=jnp.int32)
    rows_live = positions[None, :] < block_sizes[:, 0:1]
    cols_live = positions[None, :] < block_sizes[:, 1:2]
    return (rows_live[:, :, None] & cols_live[:, None, :]).astype(jnp.float32)

def apply_h(vector, left_env, right_env, mpo_shift, live_mask):

    def right_side(index):
        piece = lax.dynamic_index_in_dim(vector, index, 0, keepdims=False).astype(jnp.float32)
        envir = lax.dynamic_index_in_dim(right_env, index, 0, keepdims=False).astype(jnp.float32)
        return jnp.einsum('ij,wjk->wik', piece, envir).astype(jnp.bfloat16)
    products = lax.map(right_side, jnp.arange(NL, dtype=jnp.int32))
    blank = jnp.zeros((1, W, BS, BS), jnp.bfloat16)
    padded = jnp.concatenate([blank, products, blank], axis=0)
    shifts = mpo_shift[:, None, None]

    def left_side(index):
        triple = lax.dynamic_slice_in_dim(padded, index, 3, 0)
        chosen = jnp.where(shifts == -1, triple[0], jnp.where(shifts == 0, triple[1], triple[2]))
        envir = lax.dynamic_index_in_dim(left_env, index, 0, keepdims=False)
        return jnp.einsum('wij,wjk->ik', envir.astype(jnp.float32), chosen.astype(jnp.float32))
    return live_mask * lax.map(left_side, jnp.arange(NL, dtype=jnp.int32))

def reference(psi, left_env, right_env, mpo_shift, block_sizes):
    live_mask = live_of(block_sizes)
    cells = NL * BS * BS

    def inner(left, right):
        return jnp.sum(left * right) / cells
    start = psi.astype(jnp.float32) * live_mask
    scale = jnp.sqrt(inner(start, start) + 1e-06)
    first = (start / scale).astype(jnp.bfloat16)
    first_f = first.astype(jnp.float32)
    image_one = apply_h(first, left_env, right_env, mpo_shift, live_mask)
    alpha_one = inner(first_f, image_one)
    residue = image_one - alpha_one * first_f
    beta_one = jnp.sqrt(inner(residue, residue) + 1e-06)
    second = (residue / beta_one).astype(jnp.bfloat16)
    second_f = second.astype(jnp.float32)
    image_two = apply_h(second, left_env, right_env, mpo_shift, live_mask)
    alpha_two = inner(second_f, image_two)
    residue = image_two - alpha_two * second_f - beta_one * first_f
    beta_two = jnp.sqrt(inner(residue, residue) + 1e-06)
    third = (residue / beta_two).astype(jnp.bfloat16)
    third_f = third.astype(jnp.float32)
    image_three = apply_h(third, left_env, right_env, mpo_shift, live_mask)
    alpha_three = inner(third_f, image_three)
    coefficients = jnp.stack([alpha_one, alpha_two, alpha_three, beta_one, beta_two]).astype(jnp.float32)
    return (third, image_three.astype(jnp.bfloat16), coefficients)
```

```python
import functools

import jax
import jax.numpy as jnp
from jax import lax
from jax.experimental import pallas as pl
from jax.experimental.pallas import tpu as pltpu
from jax.sharding import PartitionSpec as P

F32 = jnp.float32
BF16 = jnp.bfloat16
EPS = 1e-06


def kernel(
    n, cap, shift_ref, sizes_ref, psi_ref, left_hbm, right_hbm,
    kry_ref, img_ref, coef_ref,
    lbuf, rbuf, halo, pack, prod, where_at, nexts, u_ref, ue_ref, v_ref, ve_ref, live_ref,
    h_ref, t_ref, te_ref, part_ref, red_ref,
    load_sem, usend, urecv, hsend, hrecv, tsend, trecv, rsend, rrecv,
):
    sectors, width = psi_ref.shape[0], psi_ref.shape[1]
    count = shift_ref.shape[0]
    last = sectors - 1
    cells = float(n * sectors * width * width)
    me = lax.axis_index("site")
    has_left, has_right = me > 0, me < n - 1

    loads = []
    for i, (src, dst) in enumerate(((right_hbm, rbuf), (left_hbm, lbuf))):
        for a in range(sectors):
            copy = pltpu.make_async_copy(src.at[a], dst.at[pl.ds(a * count, count)], load_sem.at[i * sectors + a])
            copy.start()
            loads.append(copy)

    barrier = pltpu.get_barrier_semaphore()

    def greet(k, _):
        pl.semaphore_signal(
            barrier, inc=1, device_id={"site": lax.rem(me + k, n)}, device_id_type=pl.DeviceIdType.MESH
        )
        return 0

    lax.fori_loop(1, n, greet, 0)

    rows = lax.broadcasted_iota(jnp.int32, (width, width), 0)
    cols = lax.broadcasted_iota(jnp.int32, (width, width), 1)
    for a in range(sectors):
        keep = (rows < sizes_ref[a, 0]) & (cols < sizes_ref[a, 1])
        mask = jnp.where(keep, 1.0, 0.0).astype(F32)
        live_ref[a] = mask
        u_ref[a] = (psi_ref[a].astype(F32) * mask).astype(BF16)

    nl = jnp.int32(count)
    nr = jnp.int32(count)
    nexts[0, count] = nl
    nexts[1, count] = nr
    for w in range(count - 1, -1, -1):
        s = shift_ref[w]
        nexts[0, w] = nl
        nexts[1, w] = nr
        nl = jnp.where(s == -1, w, nl)
        nr = jnp.where(s == 1, w, nr)
    low = jnp.int32(sectors * count)
    high = jnp.int32(sectors * count + cap)
    for w in range(count):
        s = shift_ref[w]
        for a in range(sectors):
            place = (a + s) * count + w
            if a == 0:
                place = jnp.where(s == -1, low, place)
            if a == last:
                place = jnp.where(s == 1, high, place)
            where_at[a, w] = place
        low = low + jnp.where(s == -1, 1, 0)
        high = high + jnp.where(s == 1, 1, 0)

    @pl.when(me == 0)
    def _():
        ue_ref[0] = jnp.zeros((width, width), BF16)
        te_ref[0, 0] = jnp.zeros((width, width), F32)
        te_ref[1, 0] = jnp.zeros((width, width), F32)
        halo[0] = jnp.zeros((cap, width, width), BF16)

    @pl.when(me == n - 1)
    def _():
        ue_ref[1] = jnp.zeros((width, width), BF16)
        te_ref[0, 1] = jnp.zeros((width, width), F32)
        te_ref[1, 1] = jnp.zeros((width, width), F32)
        halo[1] = jnp.zeros((cap, width, width), BF16)

    def remote(src, dst, ssem, rsem, to):
        return pltpu.make_async_remote_copy(
            src_ref=src, dst_ref=dst, send_sem=ssem, recv_sem=rsem,
            device_id={"site": to}, device_id_type=pl.DeviceIdType.MESH,
        )

    def swap(first_src, last_src, dst, ssem, rsem):
        right = remote(last_src, dst.at[0], ssem.at[0], rsem.at[0], jnp.minimum(me + 1, n - 1))
        left = remote(first_src, dst.at[1], ssem.at[1], rsem.at[1], jnp.maximum(me - 1, 0))
        return right, left

    def start(pair):
        pl.when(has_right)(lambda: pair[0].start())
        pl.when(has_left)(lambda: pair[1].start())

    def finish(pair):
        @pl.when(has_left)
        def _():
            pair[0].wait_recv()
            pair[1].wait_send()

        @pl.when(has_right)
        def _():
            pair[1].wait_recv()
            pair[0].wait_send()

    pl.semaphore_wait(barrier, n - 1)
    u_pair = swap(u_ref.at[0], u_ref.at[last], ue_ref, usend, urecv)
    start(u_pair)

    for copy in loads[:sectors]:
        copy.wait()

    def packing(j, at):
        at_low, at_high = at
        pack[0, j] = rbuf[last * count + jnp.minimum(at_low, count - 1)]
        pack[1, j] = rbuf[jnp.minimum(at_high, count - 1)]
        return nexts[0, at_low], nexts[1, at_high]

    lax.fori_loop(0, cap, packing, (nl, nr))
    halo_pair = swap(pack.at[1], pack.at[0], halo, hsend, hrecv)
    start(halo_pair)

    group = 2 if count % 2 == 0 and cap % 2 == 0 else 1

    def products(vector, envir, base, first):
        rhs = [envir[base + first + i] for i in range(group)]
        rhs = rhs[0] if group == 1 else jnp.concatenate(rhs, axis=1)
        return jnp.dot(vector, rhs, preferred_element_type=F32).astype(BF16)

    def local_products(vec):
        def body(p, _):
            for b in range(sectors):
                out = products(vec[b], rbuf, b * count, p * group)
                for i in range(group):
                    prod[b * count + p * group + i] = out[:, i * width : (i + 1) * width]
            return 0

        lax.fori_loop(0, count // group, body, 0)

    def halo_products(vec):
        def body(p, _):
            for side in range(2):
                out = products(vec[side], halo.at[side], 0, p * group)
                for i in range(group):
                    prod[sectors * count + side * cap + p * group + i] = out[:, i * width : (i + 1) * width]
            return 0

        lax.fori_loop(0, cap // group, body, 0)

    chunk = count // 2 if count % 2 == 0 else count

    def left_side(c, _):
        for a in range(sectors):
            lhs = jnp.concatenate([lbuf[a * count + c * chunk + i] for i in range(chunk)], axis=1)
            rhs = jnp.concatenate([prod[where_at[a, c * chunk + i]] for i in range(chunk)], axis=0)
            out = jnp.dot(lhs, rhs, preferred_element_type=F32)
            h_ref[a] = h_ref[a] + out * live_ref[a]
        return 0

    def apply_left():
        h_ref[...] = jnp.zeros_like(h_ref)
        lax.fori_loop(0, count // chunk, left_side, 0)

    def flat(x):
        return x.reshape(sectors * width, width)

    def lanes(x):
        return jnp.sum(x, axis=0, keepdims=True)

    def reduce_start(step, sums):
        part_ref[step] = jnp.concatenate(
            sums + [jnp.zeros((8 - len(sums), width), F32)], axis=0
        )
        red_ref[step, me] = part_ref[step]

        def send(k, _):
            remote(
                part_ref.at[step], red_ref.at[step, me], rsend.at[step, k], rrecv.at[step, me],
                lax.rem(me + k, n),
            ).start()
            return 0

        lax.fori_loop(1, n, send, 0)

    def reduce_finish(step):
        def wait(k, _):
            j = lax.rem(me + k, n)
            got = remote(part_ref.at[step], red_ref.at[step, j], rsend.at[step, k], rrecv.at[step, j], j)
            got.wait_recv()
            got.wait_send()
            return 0

        lax.fori_loop(1, n, wait, 0)
        return [red_ref[step, :, q, :] for q in range(4)]

    def total(x):
        return jnp.sum(jnp.sum(x, axis=0, keepdims=True), axis=1, keepdims=True) / cells

    def ratio(top, bottom):
        return jnp.where(bottom > 0.0, top / jnp.where(bottom > 0.0, bottom, 1.0), 0.0)

    local_products(u_ref)
    for copy in loads[sectors:]:
        copy.wait()
    finish(u_pair)
    finish(halo_pair)
    halo_products(ue_ref)
    apply_left()
    t_pair = swap(h_ref.at[0], h_ref.at[last], te_ref.at[0], tsend.at[0], trecv.at[0])
    start(t_pair)
    u = flat(u_ref[...]).astype(F32)
    g = flat(h_ref[...])
    uu, ug = lanes(u * u), lanes(u * g)
    r = g - ratio(ug, uu) * u
    reduce_start(0, [uu, ug, lanes(r * r)])
    uu, ug, rr, _ = reduce_finish(0)
    scale2 = total(uu) + EPS
    inv_scale = lax.rsqrt(scale2)
    alpha1 = total(ug) / scale2
    off = ratio(ug, uu) - alpha1
    beta1 = jnp.sqrt(total(rr + off * off * uu) / scale2 + EPS)
    down = inv_scale / beta1
    finish(t_pair)
    for a in range(sectors):
        v_ref[a] = ((h_ref[a] - alpha1 * u_ref[a].astype(F32)) * down).astype(BF16)
    for side in range(2):
        ve_ref[side] = ((te_ref[0, side] - alpha1 * ue_ref[side].astype(F32)) * down).astype(BF16)

    local_products(v_ref)
    halo_products(ve_ref)
    apply_left()
    v = flat(v_ref[...]).astype(F32)
    h = flat(h_ref[...])
    t = h - (beta1 * inv_scale) * flat(u_ref[...]).astype(F32)
    t_ref[...] = t.reshape(t_ref.shape)
    t_pair = swap(t_ref.at[0], t_ref.at[last], te_ref.at[1], tsend.at[1], trecv.at[1])
    start(t_pair)
    vv, vh, vt = lanes(v * v), lanes(v * h), lanes(v * t)
    r = t - ratio(vt, vv) * v
    reduce_start(1, [vv, vh, vt, lanes(r * r)])
    vv, vh, vt, rr = reduce_finish(1)
    alpha2 = total(vh)
    off = ratio(vt, vv) - alpha2
    beta2 = jnp.sqrt(total(rr + off * off * vv) + EPS)
    down = 1.0 / beta2
    finish(t_pair)
    for a in range(sectors):
        kry_ref[a] = ((t_ref[a] - alpha2 * v_ref[a].astype(F32)) * down).astype(BF16)
    for side in range(2):
        ve_ref[side] = ((te_ref[1, side] - alpha2 * ve_ref[side].astype(F32)) * down).astype(BF16)

    local_products(kry_ref)
    halo_products(ve_ref)
    apply_left()
    reduce_start(2, [lanes(flat(kry_ref[...]).astype(F32) * flat(h_ref[...]))])
    img_ref[...] = h_ref[...].astype(BF16)
    alpha3 = total(reduce_finish(2)[0])
    lane = lax.broadcasted_iota(jnp.int32, coef_ref.shape, 1)
    out = jnp.zeros(coef_ref.shape, F32)
    for i, value in enumerate((alpha1, alpha2, alpha3, beta1, beta2)):
        out = jnp.where(lane == i, value, out)
    coef_ref[...] = out


def call(n, cap, collective, psi, left_env, right_env, mpo_shift, block_sizes):
    sectors, width = psi.shape[0], psi.shape[1]
    count = mpo_shift.shape[0]
    vmem = pl.BlockSpec(memory_space=pltpu.VMEM)
    smem = pl.BlockSpec(memory_space=pltpu.SMEM)
    hbm = pl.BlockSpec(memory_space=pl.ANY)
    block = (width, width)
    dma = pltpu.SemaphoreType.DMA
    return pl.pallas_call(
        functools.partial(kernel, n, cap),
        out_shape=(
            jax.ShapeDtypeStruct(psi.shape, BF16),
            jax.ShapeDtypeStruct(psi.shape, BF16),
            jax.ShapeDtypeStruct((1, width), F32),
        ),
        in_specs=[smem, smem, vmem, hbm, hbm],
        out_specs=(vmem, vmem, vmem),
        scratch_shapes=[
            pltpu.VMEM((sectors * count,) + block, BF16),
            pltpu.VMEM((sectors * count,) + block, BF16),
            pltpu.VMEM((2, cap) + block, BF16),
            pltpu.VMEM((2, cap) + block, BF16),
            pltpu.VMEM((sectors * count + 2 * cap,) + block, BF16),
            pltpu.SMEM((sectors, count), jnp.int32),
            pltpu.SMEM((2, count + 1), jnp.int32),
            pltpu.VMEM((sectors,) + block, BF16),
            pltpu.VMEM((2,) + block, BF16),
            pltpu.VMEM((sectors,) + block, BF16),
            pltpu.VMEM((2,) + block, BF16),
            pltpu.VMEM((sectors,) + block, F32),
            pltpu.VMEM((sectors,) + block, F32),
            pltpu.VMEM((sectors,) + block, F32),
            pltpu.VMEM((2, 2) + block, F32),
            pltpu.VMEM((3, 8, width), F32),
            pltpu.VMEM((3, n, 8, width), F32),
            dma((2 * sectors,)),
            dma((2,)), dma((2,)), dma((2,)), dma((2,)),
            dma((2, 2)), dma((2, 2)),
            dma((3, n)), dma((3, n)),
        ],
        compiler_params=pltpu.CompilerParams(
            collective_id=collective, has_side_effects=True, vmem_limit_bytes=56 * 1024 * 1024
        ),
    )(mpo_shift, block_sizes, psi, left_env, right_env)


def shards(n, psi, left_env, right_env, mpo_shift, block_sizes):
    count = mpo_shift.shape[0]
    krylov, image, coefficients = call(n, count, 0, psi, left_env, right_env, mpo_shift, block_sizes)
    return krylov, image, coefficients[0, :5]


def solution(mesh):
    in_specs = (
        P(("grp", "site"), None, None),
        P(("grp", "site"), None, None, None),
        P(("grp", "site"), None, None, None),
        P(),
        P(("grp", "site"), None),
    )
    out_specs = (P(("grp", "site"), None, None), P(("grp", "site"), None, None), P("grp"))
    return jax.shard_map(
        functools.partial(shards, mesh.shape["site"]),
        mesh=mesh, in_specs=in_specs, out_specs=out_specs, check_vma=False,
    )
```

```python
import functools

import jax
import jax.numpy as jnp
from jax import lax
from jax.experimental import pallas as pl
from jax.experimental.pallas import tpu as pltpu
from jax.sharding import PartitionSpec as P

F32 = jnp.float32
BF16 = jnp.bfloat16
EPS = 1e-06
PIECE = 6


def kernel(
    n, cap, shift_ref, sizes_ref, psi_ref, left_hbm, right_hbm,
    kry_ref, img_ref, coef_ref,
    lbuf, rbuf, edge, halo, pack, prod, where_at, nexts, u_ref, ue_ref, v_ref, ve_ref, live_ref,
    h_ref, t_ref, te_ref, part_ref, red_ref,
    load_sem, edge_sem, usend, urecv, hsend, hrecv, tsend, trecv, rsend, rrecv,
):
    sectors, width = psi_ref.shape[0], psi_ref.shape[1]
    count = shift_ref.shape[0]
    last = sectors - 1
    cells = float(n * sectors * width * width)
    me = lax.axis_index("site")
    has_left, has_right = me > 0, me < n - 1

    edges = []
    for side, sector in enumerate((last, 0)):
        copy = pltpu.make_async_copy(right_hbm.at[sector], edge.at[pl.ds(side * count, count)], edge_sem.at[side])
        copy.start()
        edges.append(copy)
    loads = []
    for i, (src, dst) in enumerate(((right_hbm, rbuf), (left_hbm, lbuf))):
        for a in range(sectors):
            copy = pltpu.make_async_copy(src.at[a], dst.at[pl.ds(a * count, count)], load_sem.at[i * sectors + a])
            copy.start()
            loads.append(copy)

    barrier = pltpu.get_barrier_semaphore()

    def greet(k, _):
        pl.semaphore_signal(
            barrier, inc=1, device_id={"site": lax.rem(me + k, n)}, device_id_type=pl.DeviceIdType.MESH
        )
        return 0

    lax.fori_loop(1, n, greet, 0)

    rows = lax.broadcasted_iota(jnp.int32, (width, width), 0)
    cols = lax.broadcasted_iota(jnp.int32, (width, width), 1)
    for a in range(sectors):
        keep = (rows < sizes_ref[0:1, a : a + 1]) & (cols < sizes_ref[1:2, a : a + 1])
        mask = jnp.where(keep, 1.0, 0.0).astype(F32)
        live_ref[a] = mask
        u_ref[a] = (psi_ref[a].astype(F32) * mask).astype(BF16)

    nl = jnp.int32(count)
    nr = jnp.int32(count)
    nexts[0, count] = nl
    nexts[1, count] = nr
    for w in range(count - 1, -1, -1):
        s = shift_ref[w]
        nexts[0, w] = nl
        nexts[1, w] = nr
        nl = jnp.where(s == -1, w, nl)
        nr = jnp.where(s == 1, w, nr)
    low = jnp.int32(sectors * count)
    high = jnp.int32(sectors * count + cap)
    for w in range(count):
        s = shift_ref[w]
        for a in range(sectors):
            place = (a + s) * count + w
            if a == 0:
                place = jnp.where(s == -1, low, place)
            if a == last:
                place = jnp.where(s == 1, high, place)
            where_at[a, w] = place
        low = low + jnp.where(s == -1, 1, 0)
        high = high + jnp.where(s == 1, 1, 0)

    @pl.when(me == 0)
    def _():
        ue_ref[0] = jnp.zeros((width, width), BF16)
        te_ref[0, 0] = jnp.zeros((width, width), F32)
        te_ref[1, 0] = jnp.zeros((width, width), F32)
        halo[0] = jnp.zeros((cap, width, width), BF16)

    @pl.when(me == n - 1)
    def _():
        ue_ref[1] = jnp.zeros((width, width), BF16)
        te_ref[0, 1] = jnp.zeros((width, width), F32)
        te_ref[1, 1] = jnp.zeros((width, width), F32)
        halo[1] = jnp.zeros((cap, width, width), BF16)

    def remote(src, dst, ssem, rsem, to):
        return pltpu.make_async_remote_copy(
            src_ref=src, dst_ref=dst, send_sem=ssem, recv_sem=rsem,
            device_id={"site": to}, device_id_type=pl.DeviceIdType.MESH,
        )

    def swap(first_src, last_src, dst, ssem, rsem):
        right = remote(last_src, dst.at[0], ssem.at[0], rsem.at[0], jnp.minimum(me + 1, n - 1))
        left = remote(first_src, dst.at[1], ssem.at[1], rsem.at[1], jnp.maximum(me - 1, 0))
        return right, left

    def start(pair):
        pl.when(has_right)(lambda: pair[0].start())
        pl.when(has_left)(lambda: pair[1].start())

    def finish(pair):
        @pl.when(has_left)
        def _():
            pair[0].wait_recv()
            pair[1].wait_send()

        @pl.when(has_right)
        def _():
            pair[1].wait_recv()
            pair[0].wait_send()

    for copy in edges:
        copy.wait()

    def packing(j, at):
        at_low, at_high = at
        pack[0, j] = edge[jnp.minimum(at_low, count - 1)]
        pack[1, j] = edge[count + jnp.minimum(at_high, count - 1)]
        return nexts[0, at_low], nexts[1, at_high]

    at = (nl, nr)
    pieces = []
    for i, begin in enumerate(range(0, cap, PIECE)):
        size = min(PIECE, cap - begin)
        at = lax.fori_loop(begin, begin + size, packing, at)
        if i == 0:
            pl.semaphore_wait(barrier, n - 1)
        some = pl.ds(begin, size)
        right = remote(
            pack.at[0, some], halo.at[0, some], hsend.at[0, i], hrecv.at[0, i], jnp.minimum(me + 1, n - 1)
        )
        left = remote(
            pack.at[1, some], halo.at[1, some], hsend.at[1, i], hrecv.at[1, i], jnp.maximum(me - 1, 0)
        )
        start((right, left))
        if i == 0:
            u_pair = swap(u_ref.at[0], u_ref.at[last], ue_ref, usend, urecv)
            start(u_pair)
        pieces.append((begin, size, (right, left)))

    group = 2 if count % 2 == 0 and cap % 2 == 0 else 1

    def products(vector, envir, base, first):
        rhs = [envir[base + first + i] for i in range(group)]
        rhs = rhs[0] if group == 1 else jnp.concatenate(rhs, axis=1)
        return jnp.dot(vector, rhs, preferred_element_type=F32).astype(BF16)

    def local_products(vec):
        def body(p, _):
            for b in range(sectors):
                out = products(vec[b], rbuf, b * count, p * group)
                for i in range(group):
                    prod[b * count + p * group + i] = out[:, i * width : (i + 1) * width]
            return 0

        lax.fori_loop(0, count // group, body, 0)

    def halo_products(vec, begin=0, size=cap):
        def body(p, _):
            for side in range(2):
                out = products(vec[side], halo.at[side], 0, p * group)
                for i in range(group):
                    prod[sectors * count + side * cap + p * group + i] = out[:, i * width : (i + 1) * width]
            return 0

        lax.fori_loop(begin // group, (begin + size) // group, body, 0)

    chunk = count // 2 if count % 2 == 0 else count

    def left_side(places, c, _):
        for a in places:
            lhs = jnp.concatenate([lbuf[a * count + c * chunk + i] for i in range(chunk)], axis=1)
            rhs = jnp.concatenate([prod[where_at[a, c * chunk + i]] for i in range(chunk)], axis=0)
            out = jnp.dot(lhs, rhs, preferred_element_type=F32)
            h_ref[a] = h_ref[a] + out * live_ref[a]
        return 0

    def apply_left(places=tuple(range(sectors))):
        for a in places:
            h_ref[a] = jnp.zeros((width, width), F32)
        lax.fori_loop(0, count // chunk, functools.partial(left_side, places), 0)

    def flat(x):
        return x.reshape(sectors * width, width)

    def lanes(x):
        return jnp.sum(x, axis=0, keepdims=True)

    def reduce_start(step, sums):
        part_ref[step] = jnp.concatenate(
            sums + [jnp.zeros((8 - len(sums), width), F32)], axis=0
        )
        red_ref[step, me] = part_ref[step]

        def send(k, _):
            remote(
                part_ref.at[step], red_ref.at[step, me], rsend.at[step, k], rrecv.at[step, me],
                lax.rem(me + k, n),
            ).start()
            return 0

        lax.fori_loop(1, n, send, 0)

    def reduce_finish(step):
        def wait(k, _):
            j = lax.rem(me + k, n)
            got = remote(part_ref.at[step], red_ref.at[step, j], rsend.at[step, k], rrecv.at[step, j], j)
            got.wait_recv()
            got.wait_send()
            return 0

        lax.fori_loop(1, n, wait, 0)
        return [red_ref[step, :, q, :] for q in range(4)]

    def total(x):
        return jnp.sum(jnp.sum(x, axis=0, keepdims=True), axis=1, keepdims=True) / cells

    def ratio(top, bottom):
        return jnp.where(bottom > 0.0, top / jnp.where(bottom > 0.0, bottom, 1.0), 0.0)

    for copy in loads[:sectors]:
        copy.wait()
    local_products(u_ref)
    for copy in loads[sectors:]:
        copy.wait()
    if last > 1:
        apply_left(tuple(range(1, last)))
    finish(u_pair)
    for begin, size, pair in pieces:
        finish(pair)
        halo_products(ue_ref, begin, size)
    apply_left(tuple(sorted({0, last})))
    t_pair = swap(h_ref.at[0], h_ref.at[last], te_ref.at[0], tsend.at[0], trecv.at[0])
    start(t_pair)
    u = flat(u_ref[...]).astype(F32)
    g = flat(h_ref[...])
    uu, ug = lanes(u * u), lanes(u * g)
    r = g - ratio(ug, uu) * u
    reduce_start(0, [uu, ug, lanes(r * r)])
    uu, ug, rr, _ = reduce_finish(0)
    scale2 = total(uu) + EPS
    inv_scale = lax.rsqrt(scale2)
    alpha1 = total(ug) / scale2
    off = ratio(ug, uu) - alpha1
    beta1 = jnp.sqrt(total(rr + off * off * uu) / scale2 + EPS)
    down = inv_scale / beta1
    finish(t_pair)
    for a in range(sectors):
        v_ref[a] = ((h_ref[a] - alpha1 * u_ref[a].astype(F32)) * down).astype(BF16)
    for side in range(2):
        ve_ref[side] = ((te_ref[0, side] - alpha1 * ue_ref[side].astype(F32)) * down).astype(BF16)

    local_products(v_ref)
    halo_products(ve_ref)
    apply_left()
    v = flat(v_ref[...]).astype(F32)
    h = flat(h_ref[...])
    t = h - (beta1 * inv_scale) * flat(u_ref[...]).astype(F32)
    t_ref[...] = t.reshape(t_ref.shape)
    t_pair = swap(t_ref.at[0], t_ref.at[last], te_ref.at[1], tsend.at[1], trecv.at[1])
    start(t_pair)
    vv, vh, vt = lanes(v * v), lanes(v * h), lanes(v * t)
    r = t - ratio(vt, vv) * v
    reduce_start(1, [vv, vh, vt, lanes(r * r)])
    vv, vh, vt, rr = reduce_finish(1)
    alpha2 = total(vh)
    off = ratio(vt, vv) - alpha2
    beta2 = jnp.sqrt(total(rr + off * off * vv) + EPS)
    down = 1.0 / beta2
    finish(t_pair)
    for a in range(sectors):
        kry_ref[a] = ((t_ref[a] - alpha2 * v_ref[a].astype(F32)) * down).astype(BF16)
    for side in range(2):
        ve_ref[side] = ((te_ref[1, side] - alpha2 * ve_ref[side].astype(F32)) * down).astype(BF16)

    local_products(kry_ref)
    halo_products(ve_ref)
    apply_left()
    reduce_start(2, [lanes(flat(kry_ref[...]).astype(F32) * flat(h_ref[...]))])
    img_ref[...] = h_ref[...].astype(BF16)
    alpha3 = total(reduce_finish(2)[0])
    lane = lax.broadcasted_iota(jnp.int32, coef_ref.shape, 1)
    out = jnp.zeros(coef_ref.shape, F32)
    for i, value in enumerate((alpha1, alpha2, alpha3, beta1, beta2)):
        out = jnp.where(lane == i, value, out)
    coef_ref[...] = out


def call(n, cap, collective, psi, left_env, right_env, mpo_shift, block_sizes):
    sectors, width = psi.shape[0], psi.shape[1]
    count = mpo_shift.shape[0]
    vmem = pl.BlockSpec(memory_space=pltpu.VMEM)
    smem = pl.BlockSpec(memory_space=pltpu.SMEM)
    hbm = pl.BlockSpec(memory_space=pl.ANY)
    block = (width, width)
    dma = pltpu.SemaphoreType.DMA
    pieces = -(-cap // PIECE)
    return pl.pallas_call(
        functools.partial(kernel, n, cap),
        out_shape=(
            jax.ShapeDtypeStruct(psi.shape, BF16),
            jax.ShapeDtypeStruct(psi.shape, BF16),
            jax.ShapeDtypeStruct((1, width), F32),
        ),
        in_specs=[smem, vmem, vmem, hbm, hbm],
        out_specs=(vmem, vmem, vmem),
        scratch_shapes=[
            pltpu.VMEM((sectors * count,) + block, BF16),
            pltpu.VMEM((sectors * count,) + block, BF16),
            pltpu.VMEM((2 * count,) + block, BF16),
            pltpu.VMEM((2, cap) + block, BF16),
            pltpu.VMEM((2, cap) + block, BF16),
            pltpu.VMEM((sectors * count + 2 * cap,) + block, BF16),
            pltpu.SMEM((sectors, count), jnp.int32),
            pltpu.SMEM((2, count + 1), jnp.int32),
            pltpu.VMEM((sectors,) + block, BF16),
            pltpu.VMEM((2,) + block, BF16),
            pltpu.VMEM((sectors,) + block, BF16),
            pltpu.VMEM((2,) + block, BF16),
            pltpu.VMEM((sectors,) + block, F32),
            pltpu.VMEM((sectors,) + block, F32),
            pltpu.VMEM((sectors,) + block, F32),
            pltpu.VMEM((2, 2) + block, F32),
            pltpu.VMEM((3, 8, width), F32),
            pltpu.VMEM((3, n, 8, width), F32),
            dma((2 * sectors,)),
            dma((2,)), dma((2,)), dma((2,)),
            dma((2, pieces)), dma((2, pieces)),
            dma((2, 2)), dma((2, 2)),
            dma((3, n)), dma((3, n)),
        ],
        compiler_params=pltpu.CompilerParams(
            collective_id=collective, has_side_effects=True, vmem_limit_bytes=56 * 1024 * 1024
        ),
    )(mpo_shift, block_sizes, psi, left_env, right_env)


def write_out(kry_in, img_in, coef_in, kry_ref, img_ref, coef_ref):
    kry_ref[...] = kry_in[...]
    img_ref[...] = img_in[...]
    for i in range(coef_ref.shape[0]):
        coef_ref[i] = coef_in[0, i]


def shards(n, psi, left_env, right_env, mpo_shift, block_sizes):
    count = mpo_shift.shape[0]
    args = (psi, left_env, right_env, mpo_shift, block_sizes.T)
    caps = sorted({min(14, count), min(18, count), count})
    most = jnp.maximum(jnp.sum(mpo_shift == -1), jnp.sum(mpo_shift == 1))
    which = sum((most > cap).astype(jnp.int32) for cap in caps[:-1])
    branches = [functools.partial(call, n, cap, i) for i, cap in enumerate(caps)]
    krylov, image, coefficients = lax.switch(which, branches, *args)
    vmem = pl.BlockSpec(memory_space=pltpu.VMEM)
    return pl.pallas_call(
        write_out,
        out_shape=(
            jax.ShapeDtypeStruct(psi.shape, BF16),
            jax.ShapeDtypeStruct(psi.shape, BF16),
            jax.ShapeDtypeStruct((5,), F32),
        ),
        in_specs=[vmem] * 3,
        out_specs=(vmem, vmem, pl.BlockSpec(memory_space=pltpu.SMEM)),
    )(krylov, image, coefficients)


def solution(mesh):
    in_specs = (
        P(("grp", "site"), None, None),
        P(("grp", "site"), None, None, None),
        P(("grp", "site"), None, None, None),
        P(),
        P(("grp", "site"), None),
    )
    out_specs = (P(("grp", "site"), None, None), P(("grp", "site"), None, None), P("grp"))
    return jax.shard_map(
        functools.partial(shards, mesh.shape["site"]),
        mesh=mesh, in_specs=in_specs, out_specs=out_specs, check_vma=False,
    )
```

```python
import functools

import jax
import jax.numpy as jnp
from jax import lax
from jax.experimental import pallas as pl
from jax.experimental.pallas import tpu as pltpu
from jax.sharding import PartitionSpec as P

F32 = jnp.float32
BF16 = jnp.bfloat16
EPS = 1e-06
PIECE = 6


def kernel(
    n, cap, shift_ref, sizes_ref, psi_ref, left_hbm, right_hbm,
    kry_ref, img_ref, coef_ref,
    lbuf, rbuf, edge, halo, pack, prod, where_at, nexts, u_ref, ue_ref, v_ref, ve_ref, live_ref,
    h_ref, t_ref, te_ref, part_ref, red_ref,
    load_sem, edge_sem, usend, urecv, hsend, hrecv, tsend, trecv, rsend, rrecv,
):
    sectors, width = psi_ref.shape[0], psi_ref.shape[1]
    count = shift_ref.shape[0]
    last = sectors - 1
    cells = float(n * sectors * width * width)
    me = lax.axis_index("site")
    has_left, has_right = me > 0, me < n - 1

    edges = []
    for side, sector in enumerate((last, 0)):
        copy = pltpu.make_async_copy(right_hbm.at[sector], edge.at[pl.ds(side * count, count)], edge_sem.at[side])
        copy.start()
        edges.append(copy)
    loads = []
    for i, (src, dst) in enumerate(((right_hbm, rbuf), (left_hbm, lbuf))):
        for a in range(sectors):
            copy = pltpu.make_async_copy(src.at[a], dst.at[pl.ds(a * count, count)], load_sem.at[i * sectors + a])
            copy.start()
            loads.append(copy)

    barrier = pltpu.get_barrier_semaphore()

    def greet(k, _):
        pl.semaphore_signal(
            barrier, inc=1, device_id={"site": lax.rem(me + k, n)}, device_id_type=pl.DeviceIdType.MESH
        )
        return 0

    lax.fori_loop(1, n, greet, 0)

    nl = jnp.int32(count)
    nr = jnp.int32(count)
    nexts[0, count] = nl
    nexts[1, count] = nr
    for w in range(count - 1, -1, -1):
        s = shift_ref[w]
        nexts[0, w] = nl
        nexts[1, w] = nr
        nl = jnp.where(s == -1, w, nl)
        nr = jnp.where(s == 1, w, nr)
    def remote(src, dst, ssem, rsem, to):
        return pltpu.make_async_remote_copy(
            src_ref=src, dst_ref=dst, send_sem=ssem, recv_sem=rsem,
            device_id={"site": to}, device_id_type=pl.DeviceIdType.MESH,
        )

    def swap(first_src, last_src, dst, ssem, rsem):
        right = remote(last_src, dst.at[0], ssem.at[0], rsem.at[0], jnp.minimum(me + 1, n - 1))
        left = remote(first_src, dst.at[1], ssem.at[1], rsem.at[1], jnp.maximum(me - 1, 0))
        return right, left

    def start(pair):
        pl.when(has_right)(lambda: pair[0].start())
        pl.when(has_left)(lambda: pair[1].start())

    def finish(pair):
        @pl.when(has_left)
        def _():
            pair[0].wait_recv()
            pair[1].wait_send()

        @pl.when(has_right)
        def _():
            pair[1].wait_recv()
            pair[0].wait_send()

    rows = lax.broadcasted_iota(jnp.int32, (width, width), 0)
    cols = lax.broadcasted_iota(jnp.int32, (width, width), 1)
    for a in range(sectors):
        keep = (rows < sizes_ref[0:1, a : a + 1]) & (cols < sizes_ref[1:2, a : a + 1])
        mask = jnp.where(keep, 1.0, 0.0).astype(F32)
        live_ref[a] = mask
        u_ref[a] = (psi_ref[a].astype(F32) * mask).astype(BF16)

    for copy in edges:
        copy.wait()

    def packing(j, at):
        at_low, at_high = at
        pack[0, j] = edge[jnp.minimum(at_low, count - 1)]
        pack[1, j] = edge[count + jnp.minimum(at_high, count - 1)]
        return nexts[0, at_low], nexts[1, at_high]

    at = (nl, nr)
    pieces = []
    for i, begin in enumerate(range(0, cap, PIECE)):
        size = min(PIECE, cap - begin)
        at = lax.fori_loop(begin, begin + size, packing, at)
        if i == 0:
            pl.semaphore_wait(barrier, n - 1)
            u_pair = swap(u_ref.at[0], u_ref.at[last], ue_ref, usend, urecv)
            start(u_pair)
        some = pl.ds(begin, size)
        right = remote(
            pack.at[0, some], halo.at[0, some], hsend.at[0, i], hrecv.at[0, i], jnp.minimum(me + 1, n - 1)
        )
        left = remote(
            pack.at[1, some], halo.at[1, some], hsend.at[1, i], hrecv.at[1, i], jnp.maximum(me - 1, 0)
        )
        start((right, left))
        pieces.append((begin, size, (right, left)))

    low = jnp.int32(sectors * count)
    high = jnp.int32(sectors * count + cap)
    for w in range(count):
        s = shift_ref[w]
        for a in range(sectors):
            place = (a + s) * count + w
            if a == 0:
                place = jnp.where(s == -1, low, place)
            if a == last:
                place = jnp.where(s == 1, high, place)
            where_at[a, w] = place
        low = low + jnp.where(s == -1, 1, 0)
        high = high + jnp.where(s == 1, 1, 0)

    @pl.when(me == 0)
    def _():
        ue_ref[0] = jnp.zeros((width, width), BF16)
        te_ref[0, 0] = jnp.zeros((width, width), F32)
        te_ref[1, 0] = jnp.zeros((width, width), F32)
        halo[0] = jnp.zeros((cap, width, width), BF16)

    @pl.when(me == n - 1)
    def _():
        ue_ref[1] = jnp.zeros((width, width), BF16)
        te_ref[0, 1] = jnp.zeros((width, width), F32)
        te_ref[1, 1] = jnp.zeros((width, width), F32)
        halo[1] = jnp.zeros((cap, width, width), BF16)


    group = 2 if count % 2 == 0 and cap % 2 == 0 else 1

    def products(vector, envir, base, first):
        rhs = [envir[base + first + i] for i in range(group)]
        rhs = rhs[0] if group == 1 else jnp.concatenate(rhs, axis=1)
        return jnp.dot(vector, rhs, preferred_element_type=F32).astype(BF16)

    def local_products(vec):
        def body(p, _):
            for b in range(sectors):
                out = products(vec[b], rbuf, b * count, p * group)
                for i in range(group):
                    prod[b * count + p * group + i] = out[:, i * width : (i + 1) * width]
            return 0

        lax.fori_loop(0, count // group, body, 0)

    def halo_products(vec, begin=0, size=cap):
        def body(p, _):
            for side in range(2):
                out = products(vec[side], halo.at[side], 0, p * group)
                for i in range(group):
                    prod[sectors * count + side * cap + p * group + i] = out[:, i * width : (i + 1) * width]
            return 0

        lax.fori_loop(begin // group, (begin + size) // group, body, 0)

    chunk = count // 2 if count % 2 == 0 else count

    def left_side(places, c, _):
        for a in places:
            lhs = jnp.concatenate([lbuf[a * count + c * chunk + i] for i in range(chunk)], axis=1)
            rhs = jnp.concatenate([prod[where_at[a, c * chunk + i]] for i in range(chunk)], axis=0)
            out = jnp.dot(lhs, rhs, preferred_element_type=F32)
            h_ref[a] = h_ref[a] + out * live_ref[a]
        return 0

    def apply_left(places):
        for a in places:
            h_ref[a] = jnp.zeros((width, width), F32)
        lax.fori_loop(0, count // chunk, functools.partial(left_side, places), 0)

    def flat(x):
        return x.reshape(sectors * width, width)

    def summed(x):
        return jnp.sum(jnp.sum(x, axis=0, keepdims=True), axis=1, keepdims=True)

    def reduce_start(step, sums):
        at = lax.broadcasted_iota(jnp.int32, (1, width), 1)
        row = jnp.zeros((1, width), F32)
        for q, value in enumerate(sums):
            row = jnp.where(at == q, value, row)
        part_ref[step] = row
        red_ref[step, me] = row

        def send(k, _):
            remote(
                part_ref.at[step], red_ref.at[step, me], rsend.at[step, k], rrecv.at[step, me],
                lax.rem(me + k, n),
            ).start()
            return 0

        lax.fori_loop(1, n, send, 0)

    def reduce_finish(step):
        def wait(k, _):
            j = lax.rem(me + k, n)
            got = remote(part_ref.at[step], red_ref.at[step, j], rsend.at[step, k], rrecv.at[step, j], j)
            got.wait_recv()
            got.wait_send()
            return 0

        lax.fori_loop(1, n, wait, 0)
        got = red_ref[step].reshape(n, width)
        return [got[:, q : q + 1] for q in range(4)]

    def total(x):
        return jnp.sum(x, axis=0, keepdims=True) / cells

    def ratio(top, bottom):
        return jnp.where(bottom > 0.0, top / jnp.where(bottom > 0.0, bottom, 1.0), 0.0)

    for copy in loads[:sectors]:
        copy.wait()
    local_products(u_ref)
    for copy in loads[sectors:]:
        copy.wait()
    inner, outer = tuple(range(1, last)), tuple(sorted({0, last}))
    if inner:
        apply_left(inner)
    finish(u_pair)
    for begin, size, pair in pieces:
        finish(pair)
        halo_products(ue_ref, begin, size)
    apply_left(outer)
    u = flat(u_ref[...]).astype(F32)
    g = flat(h_ref[...])
    uu, ug = summed(u * u), summed(u * g)
    r = g - ratio(ug, uu) * u
    reduce_start(0, [uu, ug, summed(r * r)])
    t_pair = swap(h_ref.at[0], h_ref.at[last], te_ref.at[0], tsend.at[0], trecv.at[0])
    start(t_pair)
    uu, ug, rr, _ = reduce_finish(0)
    scale2 = total(uu) + EPS
    inv_scale = lax.rsqrt(scale2)
    alpha1 = total(ug) / scale2
    off = ratio(ug, uu) - alpha1
    beta1 = jnp.sqrt(total(rr + off * off * uu) / scale2 + EPS)
    down = inv_scale / beta1
    for a in range(sectors):
        v_ref[a] = ((h_ref[a] - alpha1 * u_ref[a].astype(F32)) * down).astype(BF16)

    local_products(v_ref)
    if inner:
        apply_left(inner)
    finish(t_pair)
    for side in range(2):
        ve_ref[side] = ((te_ref[0, side] - alpha1 * ue_ref[side].astype(F32)) * down).astype(BF16)
    halo_products(ve_ref)
    apply_left(outer)
    v = flat(v_ref[...]).astype(F32)
    h = flat(h_ref[...])
    t = h - (beta1 * inv_scale) * flat(u_ref[...]).astype(F32)
    t_ref[...] = t.reshape(t_ref.shape)
    vv, vh, vt = summed(v * v), summed(v * h), summed(v * t)
    r = t - ratio(vt, vv) * v
    reduce_start(1, [vv, vh, vt, summed(r * r)])
    t_pair = swap(t_ref.at[0], t_ref.at[last], te_ref.at[1], tsend.at[1], trecv.at[1])
    start(t_pair)
    vv, vh, vt, rr = reduce_finish(1)
    alpha2 = total(vh)
    off = ratio(vt, vv) - alpha2
    beta2 = jnp.sqrt(total(rr + off * off * vv) + EPS)
    down = 1.0 / beta2
    for a in range(sectors):
        kry_ref[a] = ((t_ref[a] - alpha2 * v_ref[a].astype(F32)) * down).astype(BF16)

    local_products(kry_ref)
    if inner:
        apply_left(inner)
    finish(t_pair)
    for side in range(2):
        ve_ref[side] = ((te_ref[1, side] - alpha2 * ve_ref[side].astype(F32)) * down).astype(BF16)
    halo_products(ve_ref)
    apply_left(outer)
    reduce_start(2, [summed(flat(kry_ref[...]).astype(F32) * flat(h_ref[...]))])
    img_ref[...] = h_ref[...].astype(BF16)
    alpha3 = total(reduce_finish(2)[0])
    lane = lax.broadcasted_iota(jnp.int32, coef_ref.shape, 1)
    out = jnp.zeros(coef_ref.shape, F32)
    for i, value in enumerate((alpha1, alpha2, alpha3, beta1, beta2)):
        out = jnp.where(lane == i, value, out)
    coef_ref[...] = out


def call(n, cap, collective, psi, left_env, right_env, mpo_shift, block_sizes):
    sectors, width = psi.shape[0], psi.shape[1]
    count = mpo_shift.shape[0]
    vmem = pl.BlockSpec(memory_space=pltpu.VMEM)
    smem = pl.BlockSpec(memory_space=pltpu.SMEM)
    hbm = pl.BlockSpec(memory_space=pl.ANY)
    block = (width, width)
    dma = pltpu.SemaphoreType.DMA
    pieces = -(-cap // PIECE)
    return pl.pallas_call(
        functools.partial(kernel, n, cap),
        out_shape=(
            jax.ShapeDtypeStruct(psi.shape, BF16),
            jax.ShapeDtypeStruct(psi.shape, BF16),
            jax.ShapeDtypeStruct((1, width), F32),
        ),
        in_specs=[smem, vmem, vmem, hbm, hbm],
        out_specs=(vmem, vmem, vmem),
        scratch_shapes=[
            pltpu.VMEM((sectors * count,) + block, BF16),
            pltpu.VMEM((sectors * count,) + block, BF16),
            pltpu.VMEM((2 * count,) + block, BF16),
            pltpu.VMEM((2, cap) + block, BF16),
            pltpu.VMEM((2, cap) + block, BF16),
            pltpu.VMEM((sectors * count + 2 * cap,) + block, BF16),
            pltpu.SMEM((sectors, count), jnp.int32),
            pltpu.SMEM((2, count + 1), jnp.int32),
            pltpu.VMEM((sectors,) + block, BF16),
            pltpu.VMEM((2,) + block, BF16),
            pltpu.VMEM((sectors,) + block, BF16),
            pltpu.VMEM((2,) + block, BF16),
            pltpu.VMEM((sectors,) + block, F32),
            pltpu.VMEM((sectors,) + block, F32),
            pltpu.VMEM((sectors,) + block, F32),
            pltpu.VMEM((2, 2) + block, F32),
            pltpu.VMEM((3, 1, width), F32),
            pltpu.VMEM((3, n, 1, width), F32),
            dma((2 * sectors,)),
            dma((2,)), dma((2,)), dma((2,)),
            dma((2, pieces)), dma((2, pieces)),
            dma((2, 2)), dma((2, 2)),
            dma((3, n)), dma((3, n)),
        ],
        compiler_params=pltpu.CompilerParams(
            collective_id=collective, has_side_effects=True, vmem_limit_bytes=56 * 1024 * 1024
        ),
    )(mpo_shift, block_sizes, psi, left_env, right_env)


def write_out(kry_in, img_in, coef_in, kry_ref, img_ref, coef_ref):
    kry_ref[...] = kry_in[...]
    img_ref[...] = img_in[...]
    for i in range(coef_ref.shape[0]):
        coef_ref[i] = coef_in[0, i]


def shards(n, psi, left_env, right_env, mpo_shift, block_sizes):
    count = mpo_shift.shape[0]
    args = (psi, left_env, right_env, mpo_shift, block_sizes.T)
    caps = sorted({min(14, count), min(18, count), count})
    most = jnp.maximum(jnp.sum(mpo_shift == -1), jnp.sum(mpo_shift == 1))
    which = sum((most > cap).astype(jnp.int32) for cap in caps[:-1])
    branches = [functools.partial(call, n, cap, i) for i, cap in enumerate(caps)]
    krylov, image, coefficients = lax.switch(which, branches, *args)
    vmem = pl.BlockSpec(memory_space=pltpu.VMEM)
    return pl.pallas_call(
        write_out,
        out_shape=(
            jax.ShapeDtypeStruct(psi.shape, BF16),
            jax.ShapeDtypeStruct(psi.shape, BF16),
            jax.ShapeDtypeStruct((5,), F32),
        ),
        in_specs=[vmem] * 3,
        out_specs=(vmem, vmem, pl.BlockSpec(memory_space=pltpu.SMEM)),
    )(krylov, image, coefficients)


def solution(mesh):
    in_specs = (
        P(("grp", "site"), None, None),
        P(("grp", "site"), None, None, None),
        P(("grp", "site"), None, None, None),
        P(),
        P(("grp", "site"), None),
    )
    out_specs = (P(("grp", "site"), None, None), P(("grp", "site"), None, None), P("grp"))
    return jax.shard_map(
        functools.partial(shards, mesh.shape["site"]),
        mesh=mesh, in_specs=in_specs, out_specs=out_specs, check_vma=False,
    )
```

```python
import functools

import jax
import jax.numpy as jnp
from jax import lax
from jax.experimental import pallas as pl
from jax.experimental.pallas import tpu as pltpu
from jax.sharding import PartitionSpec as P

F32 = jnp.float32
BF16 = jnp.bfloat16
EPS = 1e-06
PIECE = 6


def kernel(
    n, cap, shift_ref, sizes_ref, psi_ref, left_hbm, right_hbm,
    kry_ref, img_ref, coef_ref,
    lbuf, rbuf, edge, halo, pack, prod, where_at, nexts, u_ref, ue_ref, v_ref, ve_ref, live_ref,
    h_ref, t_ref, te_ref, part_ref, red_ref,
    load_sem, edge_sem, usend, urecv, hsend, hrecv, tsend, trecv, rsend, rrecv,
):
    sectors, width = psi_ref.shape[0], psi_ref.shape[1]
    count = shift_ref.shape[0]
    last = sectors - 1
    cells = float(n * sectors * width * width)
    me = lax.axis_index("site")
    has_left, has_right = me > 0, me < n - 1
    plane = max(p for p in range(1, n + 1) if n % p == 0 and p * p <= n)
    base = me // plane * plane

    edges = []
    for side, sector in enumerate((last, 0)):
        copy = pltpu.make_async_copy(right_hbm.at[sector], edge.at[pl.ds(side * count, count)], edge_sem.at[side])
        copy.start()
        edges.append(copy)
    loads = []
    for i, (src, dst) in enumerate(((right_hbm, rbuf), (left_hbm, lbuf))):
        for a in range(sectors):
            copy = pltpu.make_async_copy(src.at[a], dst.at[pl.ds(a * count, count)], load_sem.at[i * sectors + a])
            copy.start()
            loads.append(copy)

    barrier = pltpu.get_barrier_semaphore()

    def greet(k, _):
        pl.semaphore_signal(
            barrier, inc=1, device_id={"site": lax.rem(me + k, n)}, device_id_type=pl.DeviceIdType.MESH
        )
        return 0

    lax.fori_loop(1, n, greet, 0)

    nl = jnp.int32(count)
    nr = jnp.int32(count)
    nexts[0, count] = nl
    nexts[1, count] = nr
    for w in range(count - 1, -1, -1):
        s = shift_ref[w]
        nexts[0, w] = nl
        nexts[1, w] = nr
        nl = jnp.where(s == -1, w, nl)
        nr = jnp.where(s == 1, w, nr)
    def remote(src, dst, ssem, rsem, to):
        return pltpu.make_async_remote_copy(
            src_ref=src, dst_ref=dst, send_sem=ssem, recv_sem=rsem,
            device_id={"site": to}, device_id_type=pl.DeviceIdType.MESH,
        )

    def swap(first_src, last_src, dst, ssem, rsem):
        right = remote(last_src, dst.at[0], ssem.at[0], rsem.at[0], jnp.minimum(me + 1, n - 1))
        left = remote(first_src, dst.at[1], ssem.at[1], rsem.at[1], jnp.maximum(me - 1, 0))
        return right, left

    def start(pair):
        pl.when(has_right)(lambda: pair[0].start())
        pl.when(has_left)(lambda: pair[1].start())

    def finish(pair):
        @pl.when(has_left)
        def _():
            pair[0].wait_recv()
            pair[1].wait_send()

        @pl.when(has_right)
        def _():
            pair[1].wait_recv()
            pair[0].wait_send()

    rows = lax.broadcasted_iota(jnp.int32, (width, width), 0)
    cols = lax.broadcasted_iota(jnp.int32, (width, width), 1)
    for a in range(sectors):
        keep = (rows < sizes_ref[0:1, a : a + 1]) & (cols < sizes_ref[1:2, a : a + 1])
        mask = jnp.where(keep, 1.0, 0.0).astype(F32)
        live_ref[a] = mask
        u_ref[a] = (psi_ref[a].astype(F32) * mask).astype(BF16)

    for copy in edges:
        copy.wait()

    def packing(j, at):
        at_low, at_high = at
        pack[0, j] = edge[jnp.minimum(at_low, count - 1)]
        pack[1, j] = edge[count + jnp.minimum(at_high, count - 1)]
        return nexts[0, at_low], nexts[1, at_high]

    at = (nl, nr)
    pieces = []
    for i, begin in enumerate(range(0, cap, PIECE)):
        size = min(PIECE, cap - begin)
        at = lax.fori_loop(begin, begin + size, packing, at)
        if i == 0:
            pl.semaphore_wait(barrier, n - 1)
            u_pair = swap(u_ref.at[0], u_ref.at[last], ue_ref, usend, urecv)
            start(u_pair)
        some = pl.ds(begin, size)
        right = remote(
            pack.at[0, some], halo.at[0, some], hsend.at[0, i], hrecv.at[0, i], jnp.minimum(me + 1, n - 1)
        )
        left = remote(
            pack.at[1, some], halo.at[1, some], hsend.at[1, i], hrecv.at[1, i], jnp.maximum(me - 1, 0)
        )
        start((right, left))
        pieces.append((begin, size, (right, left)))

    low = jnp.int32(sectors * count)
    high = jnp.int32(sectors * count + cap)
    for w in range(count):
        s = shift_ref[w]
        for a in range(sectors):
            place = (a + s) * count + w
            if a == 0:
                place = jnp.where(s == -1, low, place)
            if a == last:
                place = jnp.where(s == 1, high, place)
            where_at[a, w] = place
        low = low + jnp.where(s == -1, 1, 0)
        high = high + jnp.where(s == 1, 1, 0)

    @pl.when(me == 0)
    def _():
        ue_ref[0] = jnp.zeros((width, width), BF16)
        te_ref[0, 0] = jnp.zeros((width, width), F32)
        te_ref[1, 0] = jnp.zeros((width, width), F32)
        halo[0] = jnp.zeros((cap, width, width), BF16)

    @pl.when(me == n - 1)
    def _():
        ue_ref[1] = jnp.zeros((width, width), BF16)
        te_ref[0, 1] = jnp.zeros((width, width), F32)
        te_ref[1, 1] = jnp.zeros((width, width), F32)
        halo[1] = jnp.zeros((cap, width, width), BF16)


    group = 2 if count % 2 == 0 and cap % 2 == 0 else 1

    def products(vector, envir, base, first):
        rhs = [envir[base + first + i] for i in range(group)]
        rhs = rhs[0] if group == 1 else jnp.concatenate(rhs, axis=1)
        return jnp.dot(vector, rhs, preferred_element_type=F32).astype(BF16)

    def local_products(vec):
        def body(p, _):
            for b in range(sectors):
                out = products(vec[b], rbuf, b * count, p * group)
                for i in range(group):
                    prod[b * count + p * group + i] = out[:, i * width : (i + 1) * width]
            return 0

        lax.fori_loop(0, count // group, body, 0)

    def halo_products(vec, begin=0, size=cap):
        def body(p, _):
            for side in range(2):
                out = products(vec[side], halo.at[side], 0, p * group)
                for i in range(group):
                    prod[sectors * count + side * cap + p * group + i] = out[:, i * width : (i + 1) * width]
            return 0

        lax.fori_loop(begin // group, (begin + size) // group, body, 0)

    chunk = count // 2 if count % 2 == 0 else count

    def left_side(places, c, _):
        for a in places:
            lhs = jnp.concatenate([lbuf[a * count + c * chunk + i] for i in range(chunk)], axis=1)
            rhs = jnp.concatenate([prod[where_at[a, c * chunk + i]] for i in range(chunk)], axis=0)
            out = jnp.dot(lhs, rhs, preferred_element_type=F32)
            h_ref[a] = h_ref[a] + out * live_ref[a]
        return 0

    def apply_left(places):
        for a in places:
            h_ref[a] = jnp.zeros((width, width), F32)
        lax.fori_loop(0, count // chunk, functools.partial(left_side, places), 0)

    def flat(x):
        return x.reshape(sectors * width, width)

    def summed(x):
        return jnp.sum(jnp.sum(x, axis=0, keepdims=True), axis=1, keepdims=True)

    def reduce_start(step, sums):
        at = lax.broadcasted_iota(jnp.int32, (1, width), 1)
        row = jnp.zeros((1, width), F32)
        for q, value in enumerate(sums):
            row = jnp.where(at == q, value, row)
        part_ref[step] = row
        red_ref[step, me] = row

        def send(k, _):
            to = base + lax.rem(me - base + k, plane)
            remote(
                part_ref.at[step], red_ref.at[step, me], rsend.at[step, k], rrecv.at[step, me], to
            ).start()
            return 0

        lax.fori_loop(1, plane, send, 0)

    def reduce_finish(step):
        def near(k, _):
            j = base + lax.rem(me - base + k, plane)
            got = remote(part_ref.at[step], red_ref.at[step, j], rsend.at[step, k], rrecv.at[step, j], j)
            got.wait_recv()
            got.wait_send()
            return 0

        lax.fori_loop(1, plane, near, 0)

        def rows_of(j):
            return red_ref.at[step, pl.ds(j // plane * plane, plane)]

        def pass_on(m, _):
            to = lax.rem(me + m * plane, n)
            remote(
                rows_of(me), rows_of(me), rsend.at[step, plane - 1 + m], rrecv.at[step, me], to
            ).start()
            return 0

        lax.fori_loop(1, n // plane, pass_on, 0)

        def far(m, _):
            j = lax.rem(me + m * plane, n)
            got = remote(rows_of(j), rows_of(j), rsend.at[step, plane - 1 + m], rrecv.at[step, j], j)
            got.wait_recv()
            got.wait_send()
            return 0

        lax.fori_loop(1, n // plane, far, 0)
        got = red_ref[step].reshape(n, width)
        return [got[:, q : q + 1] for q in range(4)]

    def total(x):
        return jnp.sum(x, axis=0, keepdims=True) / cells

    def ratio(top, bottom):
        return jnp.where(bottom > 0.0, top / jnp.where(bottom > 0.0, bottom, 1.0), 0.0)

    for copy in loads[:sectors]:
        copy.wait()
    local_products(u_ref)
    for copy in loads[sectors:]:
        copy.wait()
    inner, outer = tuple(range(1, last)), tuple(sorted({0, last}))
    if inner:
        apply_left(inner)
    finish(u_pair)
    for begin, size, pair in pieces:
        finish(pair)
        halo_products(ue_ref, begin, size)
    apply_left(outer)
    u = flat(u_ref[...]).astype(F32)
    g = flat(h_ref[...])
    uu, ug = summed(u * u), summed(u * g)
    r = g - ratio(ug, uu) * u
    reduce_start(0, [uu, ug, summed(r * r)])
    t_pair = swap(h_ref.at[0], h_ref.at[last], te_ref.at[0], tsend.at[0], trecv.at[0])
    start(t_pair)
    uu, ug, rr, _ = reduce_finish(0)
    scale2 = total(uu) + EPS
    inv_scale = lax.rsqrt(scale2)
    alpha1 = total(ug) / scale2
    off = ratio(ug, uu) - alpha1
    beta1 = jnp.sqrt(total(rr + off * off * uu) / scale2 + EPS)
    down = inv_scale / beta1
    for a in range(sectors):
        v_ref[a] = ((h_ref[a] - alpha1 * u_ref[a].astype(F32)) * down).astype(BF16)

    local_products(v_ref)
    if inner:
        apply_left(inner)
    finish(t_pair)
    for side in range(2):
        ve_ref[side] = ((te_ref[0, side] - alpha1 * ue_ref[side].astype(F32)) * down).astype(BF16)
    halo_products(ve_ref)
    apply_left(outer)
    v = flat(v_ref[...]).astype(F32)
    h = flat(h_ref[...])
    t = h - (beta1 * inv_scale) * flat(u_ref[...]).astype(F32)
    t_ref[...] = t.reshape(t_ref.shape)
    vv, vh, vt = summed(v * v), summed(v * h), summed(v * t)
    r = t - ratio(vt, vv) * v
    reduce_start(1, [vv, vh, vt, summed(r * r)])
    t_pair = swap(t_ref.at[0], t_ref.at[last], te_ref.at[1], tsend.at[1], trecv.at[1])
    start(t_pair)
    vv, vh, vt, rr = reduce_finish(1)
    alpha2 = total(vh)
    off = ratio(vt, vv) - alpha2
    beta2 = jnp.sqrt(total(rr + off * off * vv) + EPS)
    down = 1.0 / beta2
    for a in range(sectors):
        kry_ref[a] = ((t_ref[a] - alpha2 * v_ref[a].astype(F32)) * down).astype(BF16)

    local_products(kry_ref)
    if inner:
        apply_left(inner)
    finish(t_pair)
    for side in range(2):
        ve_ref[side] = ((te_ref[1, side] - alpha2 * ve_ref[side].astype(F32)) * down).astype(BF16)
    halo_products(ve_ref)
    apply_left(outer)
    reduce_start(2, [summed(flat(kry_ref[...]).astype(F32) * flat(h_ref[...]))])
    img_ref[...] = h_ref[...].astype(BF16)
    alpha3 = total(reduce_finish(2)[0])
    lane = lax.broadcasted_iota(jnp.int32, coef_ref.shape, 1)
    out = jnp.zeros(coef_ref.shape, F32)
    for i, value in enumerate((alpha1, alpha2, alpha3, beta1, beta2)):
        out = jnp.where(lane == i, value, out)
    coef_ref[...] = out


def call(n, cap, collective, psi, left_env, right_env, mpo_shift, block_sizes):
    sectors, width = psi.shape[0], psi.shape[1]
    count = mpo_shift.shape[0]
    vmem = pl.BlockSpec(memory_space=pltpu.VMEM)
    smem = pl.BlockSpec(memory_space=pltpu.SMEM)
    hbm = pl.BlockSpec(memory_space=pl.ANY)
    block = (width, width)
    dma = pltpu.SemaphoreType.DMA
    pieces = -(-cap // PIECE)
    return pl.pallas_call(
        functools.partial(kernel, n, cap),
        out_shape=(
            jax.ShapeDtypeStruct(psi.shape, BF16),
            jax.ShapeDtypeStruct(psi.shape, BF16),
            jax.ShapeDtypeStruct((1, width), F32),
        ),
        in_specs=[smem, vmem, vmem, hbm, hbm],
        out_specs=(vmem, vmem, vmem),
        scratch_shapes=[
            pltpu.VMEM((sectors * count,) + block, BF16),
            pltpu.VMEM((sectors * count,) + block, BF16),
            pltpu.VMEM((2 * count,) + block, BF16),
            pltpu.VMEM((2, cap) + block, BF16),
            pltpu.VMEM((2, cap) + block, BF16),
            pltpu.VMEM((sectors * count + 2 * cap,) + block, BF16),
            pltpu.SMEM((sectors, count), jnp.int32),
            pltpu.SMEM((2, count + 1), jnp.int32),
            pltpu.VMEM((sectors,) + block, BF16),
            pltpu.VMEM((2,) + block, BF16),
            pltpu.VMEM((sectors,) + block, BF16),
            pltpu.VMEM((2,) + block, BF16),
            pltpu.VMEM((sectors,) + block, F32),
            pltpu.VMEM((sectors,) + block, F32),
            pltpu.VMEM((sectors,) + block, F32),
            pltpu.VMEM((2, 2) + block, F32),
            pltpu.VMEM((3, 1, width), F32),
            pltpu.VMEM((3, n, 1, width), F32),
            dma((2 * sectors,)),
            dma((2,)), dma((2,)), dma((2,)),
            dma((2, pieces)), dma((2, pieces)),
            dma((2, 2)), dma((2, 2)),
            dma((3, n)), dma((3, n)),
        ],
        compiler_params=pltpu.CompilerParams(
            collective_id=collective, has_side_effects=True, vmem_limit_bytes=56 * 1024 * 1024
        ),
    )(mpo_shift, block_sizes, psi, left_env, right_env)


def write_out(kry_in, img_in, coef_in, kry_ref, img_ref, coef_ref):
    kry_ref[...] = kry_in[...]
    img_ref[...] = img_in[...]
    for i in range(coef_ref.shape[0]):
        coef_ref[i] = coef_in[0, i]


def shards(n, psi, left_env, right_env, mpo_shift, block_sizes):
    count = mpo_shift.shape[0]
    args = (psi, left_env, right_env, mpo_shift, block_sizes.T)
    caps = sorted({min(14, count), min(18, count), count})
    most = jnp.maximum(jnp.sum(mpo_shift == -1), jnp.sum(mpo_shift == 1))
    which = sum((most > cap).astype(jnp.int32) for cap in caps[:-1])
    branches = [functools.partial(call, n, cap, i) for i, cap in enumerate(caps)]
    krylov, image, coefficients = lax.switch(which, branches, *args)
    vmem = pl.BlockSpec(memory_space=pltpu.VMEM)
    return pl.pallas_call(
        write_out,
        out_shape=(
            jax.ShapeDtypeStruct(psi.shape, BF16),
            jax.ShapeDtypeStruct(psi.shape, BF16),
            jax.ShapeDtypeStruct((5,), F32),
        ),
        in_specs=[vmem] * 3,
        out_specs=(vmem, vmem, pl.BlockSpec(memory_space=pltpu.SMEM)),
    )(krylov, image, coefficients)


def solution(mesh):
    in_specs = (
        P(("grp", "site"), None, None),
        P(("grp", "site"), None, None, None),
        P(("grp", "site"), None, None, None),
        P(),
        P(("grp", "site"), None),
    )
    out_specs = (P(("grp", "site"), None, None), P(("grp", "site"), None, None), P("grp"))
    return jax.shard_map(
        functools.partial(shards, mesh.shape["site"]),
        mesh=mesh, in_specs=in_specs, out_specs=out_specs, check_vma=False,
    )
```
